256 devices in a mesh: section: 8 (over x, core), fsdp: 32 (over y, z).
Axes of the slice: x: 4, y: 4, z: 8, core: 2. Of those that a mesh axis runs over, the one named last changes fastest.
Arguments:
- hidden: bfloat16 [512, 4608], P(('section', 'fsdp')), may hold values from -6 to 6
- unembed: bfloat16 [256000, 4608], P(('section', 'fsdp')), may hold values from -0.375 to 0.375
- targets: int32 [512], P(('section', 'fsdp')), may hold values from 0 to 255999
- valid_mask: int32 [512], P(('section', 'fsdp')), may hold values from 0 to 1, as said below
- loss_scale: float32 [], replicated, may hold values from 256 to 1024
Outputs:
- hidden_grad: float32 [512, 4608], P(('section', 'fsdp'))
- losses: float32 [4], replicated
The draws below stay inside these ranges and needn't reach their ends.
Inputs may be any that keep to these rules, and one draw needn't show every extreme that they name: `valid_mask`: the first token of every microbatch is valid.
All inputs are finite; a program needn't handle non-finite values.
Results may differ from the reference program's by a relative error of at most 0.0042.
Values may be sent and summed in bfloat16 or wider, within the bound.
No kernel may reach another device: no remote copies, remote signals or barrier semaphores. Data moves between devices by JAX's collectives and lax.ppermute only.
A program may use at most 128 MiB of HBM per device.

```python
import math
import jax
import jax.numpy as jnp
import numpy as np
from jax import lax

D = 4608
VOC_DEV = 1000
MICRO = 4
TOKENS = 512
VOCAB = 256000
N_SECTION = 8
N_FSDP = 32


def draw_valid_mask(key, part):
    tok_micro = TOKENS // MICRO
    position = jnp.arange(TOKENS, dtype=jnp.int32) % tok_micro
    threshold = 300 + 600 * position // tok_micro
    rolls = jax.random.randint(key, (TOKENS,), 0, 1000, dtype=jnp.int32)
    marks = (rolls < threshold).astype(jnp.int32)
    return jnp.where(position == 0, 1, marks).astype(jnp.int32)


def with_ends(result, own_key, low, largest):
    longest = result.shape.index(max(result.shape))
    spots = []
    for shift in (0, 1):
        where = [jax.random.randint(jax.random.fold_in(own_key, axis), (), 0, length) for axis, length in enumerate(result.shape)]
        where[longest] = (where[longest] + shift) % result.shape[longest]
        spots.append(tuple(where))
    return result.at[spots[0]].set(low).at[spots[1]].set(largest)


def block_levels(key, dims, cuts, smallest, largest):
    factor_of = 1.0
    for axis_at, shards_of in cuts:
        draws = jax.random.uniform(jax.random.fold_in(jax.random.fold_in(key, 6), axis_at), (shards_of,), jnp.float32, smallest / len(cuts), largest / len(cuts))
        factor_of = factor_of * jnp.repeat(jnp.exp(draws), dims[axis_at] // shards_of).reshape((-1,) + (1,) * (len(dims) - 1 - axis_at))
    return factor_of


def ranked_wide(rng, shape, number_of, slope):
    portions = [min(1 << octave, number_of + 1 - (1 << octave)) * (1 << 20) // math.isqrt((1 << octave) ** slope) + 1 for octave in range((number_of + 1).bit_length()) if 1 << octave <= number_of]
    spread = 1 + sum(portions) // (1 << 30)
    listing = np.cumsum(np.array([max(1, weight // spread) for weight in portions]))
    ticket = jax.random.randint(jax.random.fold_in(rng, 1), shape, 0, int(listing[len(portions) - 1]))
    start = jnp.left_shift(1, jnp.searchsorted(jnp.asarray(listing, jnp.int32), ticket, side="right").astype(jnp.int32))
    standing = start - 1 + jax.random.randint(jax.random.fold_in(rng, 4), shape, 0, 1 << 30) % jnp.minimum(start, number_of + 1 - start)
    return jax.random.permutation(jax.random.fold_in(rng, 2), number_of)[standing].astype(jnp.int32)


def scatter_about(stream_key, shape, scale, limit, cuts=(), kind=jnp.bfloat16):
    entries = scale * jax.random.normal(stream_key, shape, jnp.float32)
    if cuts:
        entries = entries * block_levels(stream_key, shape, cuts, -0.22, 0.18)
    return jnp.clip(entries, -limit, limit).astype(kind)


def setup_inputs(seed: int = 0) -> dict:
    key_list = jax.random.split(jax.random.key(seed), 6)
    hidden = scatter_about(key_list[0], (TOKENS, D), 1.0, 6.0, ((0, 256),))
    unembed = scatter_about(key_list[1], (VOCAB, D), (D // 16) ** -0.5, 0.375, ((0, 256),))
    targets = with_ends(ranked_wide(key_list[2], (TOKENS,), VOCAB, 2), jax.random.fold_in(key_list[2], 3), 0, VOCAB - 1).astype(jnp.int32)
    valid_mask = draw_valid_mask(jax.random.fold_in(key_list[5], 71), 0)
    loss_scale = jnp.clip(jnp.exp(jax.random.uniform(key_list[4], (), jnp.float32, math.log(256.0), math.log(1024.0))), 256.0, 1024.0)
    return dict(hidden=hidden, unembed=unembed, targets=targets, valid_mask=valid_mask, loss_scale=loss_scale)


SOFTCAP = 30.0


def reference(hidden, unembed, targets, valid_mask, loss_scale):
    tokens = hidden.shape[0]
    width = hidden.shape[1]
    shards = N_SECTION * N_FSDP
    rows_section = tokens // N_SECTION
    arriving = jnp.roll(hidden, rows_section, axis=0)
    blocks = unembed.reshape(shards, VOC_DEV, width)
    firsts = (jnp.arange(shards, dtype=jnp.int32) * VOC_DEV).astype(jnp.int32)

    def capped_of(block):
        logits = lax.dot_general(arriving, block, (((1,), (1,)), ((), ())), preferred_element_type=jnp.float32)
        return SOFTCAP * jnp.tanh(logits / SOFTCAP)

    def hits_of(first):
        columns = first + jnp.arange(VOC_DEV, dtype=jnp.int32)
        return columns[None, :] == targets[:, None]

    def forward(carry, item):
        block, first = item
        capped = capped_of(block)
        total = carry[0] + jnp.sum(jnp.exp(capped - SOFTCAP), axis=1)
        picked = carry[1] + jnp.sum(jnp.where(hits_of(first), capped, jnp.zeros_like(capped)), axis=1)
        return (total, picked), None

    zeros = jnp.zeros((tokens,), jnp.float32)
    (total, picked), _ = lax.scan(forward, (zeros, zeros), (blocks, firsts))
    lse = SOFTCAP + jnp.log(total)
    weights = valid_mask.astype(jnp.float32).reshape(MICRO, -1)
    counts = jnp.sum(weights, axis=1)
    losses = jnp.sum(weights * (lse - picked).reshape(MICRO, -1), axis=1) / counts
    coef = (loss_scale * weights / counts[:, None]).reshape(-1)

    def backward(carry, item):
        block, first = item
        capped = capped_of(block)
        probs = jnp.exp(capped - lse[:, None])
        onehot = hits_of(first).astype(jnp.float32)
        grad = (coef[:, None] * (probs - onehot) * (1.0 - (capped / SOFTCAP) ** 2)).astype(jnp.bfloat16)
        return carry + jnp.dot(grad, block, preferred_element_type=jnp.float32), None

    arriving_grad, _ = lax.scan(backward, jnp.zeros((tokens, width), jnp.float32), (blocks, firsts))
    hidden_grad = jnp.roll(arriving_grad, -rows_section, axis=0)
    return hidden_grad, losses
```

```python
import jax
import jax.numpy as jnp
from jax import lax
from jax.sharding import Mesh, PartitionSpec as P

MICRO = 4
SOFTCAP = 30.0
TAIL = 128
ALL = ("x", "core", "y", "z")


def swap(v):
    return lax.ppermute(v, "core", [(0, 1), (1, 0)])


def gather(v, axis):
    peers = lax.axis_size(axis)
    return lax.all_to_all(jnp.broadcast_to(v[None], (peers, *v.shape)), axis, 0, 0, tiled=True)


def body(hidden, unembed, targets, valid_mask, loss_scale):
    own_rows, width = hidden.shape
    vocab_rows = unembed.shape[0]
    nx, nc, ny, nz = (lax.axis_size(a) for a in ALL)
    core = lax.axis_index("core")
    plane = nx * ny * nz * own_rows
    f32 = jnp.float32

    unembed_sib = swap(unembed)

    digits = jnp.stack([targets % 256, (targets // 256) % 256, targets // 65536, valid_mask], axis=1)
    tail = jnp.pad(digits, ((0, 0), (0, TAIL - digits.shape[1]))).astype(jnp.bfloat16)
    mine = jnp.concatenate([hidden, tail], axis=1)
    by_z = gather(mine, "z").reshape(nz * own_rows, width + TAIL)
    rows = gather(by_z, ("x", "y")).reshape(plane, width + TAIL)
    tokens = rows[:, :width]

    own_tail = rows[:, width:]
    sib_tail = swap(own_tail)
    code_own = own_tail[:, :4].astype(jnp.int32)
    code_sib = sib_tail[:, :4].astype(jnp.int32)
    per_x = plane // nx
    code = jnp.where(core == 0, code_sib, jnp.roll(code_sib, -per_x, axis=0))
    labels = code[:, 0] + 256 * code[:, 1] + 65536 * code[:, 2]
    weights = code[:, 3].astype(f32)
    counts = jnp.sum((code_own[:, 3] + code_sib[:, 3]).reshape(nx, per_x), axis=1).astype(f32)
    counts_tok = jnp.repeat(jnp.where(core == 0, counts, jnp.roll(counts, -1)), per_x)

    def dot_t(u):
        return lax.dot_general(tokens, u, (((1,), (1,)), ((), ())), preferred_element_type=f32)

    device = lax.axis_index(ALL)
    device_sib = device + (1 - 2 * core) * ny * nz
    parts = []
    for u, d in ((unembed, device), (unembed_sib, device_sib)):
        capped = SOFTCAP * jnp.tanh(dot_t(u) / SOFTCAP)
        columns = d * vocab_rows + jnp.arange(vocab_rows, dtype=jnp.int32)
        hits = columns[None, :] == labels[:, None]
        parts.append((u, capped, hits))
    total = sum(jnp.sum(jnp.exp(c - SOFTCAP), axis=1) for _, c, _ in parts)
    picked = sum(jnp.sum(jnp.where(h, c, jnp.zeros_like(c)), axis=1) for _, c, h in parts)
    stats = jnp.stack([total, picked]).reshape(2 * plane // 128, 128)
    stats = jnp.sum(gather(stats, ("x", "y")).reshape(nx * ny, *stats.shape), axis=0)
    stats = jnp.sum(gather(stats, "z").reshape(nz, *stats.shape), axis=0)
    total, picked = stats.reshape(2, plane)

    lse = SOFTCAP + jnp.log(total)
    sums = jnp.sum((weights * (lse - picked)).reshape(nx, per_x), axis=1)
    sums = jnp.where(core == 0, sums, jnp.roll(sums, 1))
    losses = (sums + swap(sums)) / counts
    coef = loss_scale * weights / counts_tok

    partial = jnp.zeros((plane, width), f32)
    for u, capped, hits in parts:
        probs = jnp.exp(capped - lse[:, None])
        grad = coef[:, None] * (probs - hits.astype(f32)) * (1.0 - (capped / SOFTCAP) ** 2)
        partial = partial + jnp.dot(grad.astype(jnp.bfloat16), u, preferred_element_type=f32)

    cut = partial.astype(jnp.bfloat16).reshape(nx * ny, plane // (nx * ny), width)
    got = lax.all_to_all(cut, ("x", "y"), 0, 0, tiled=True)
    some = jnp.sum(got.astype(f32), axis=0)
    cut = some.astype(jnp.bfloat16).reshape(nz, own_rows, width)
    got = lax.all_to_all(cut, "z", 0, 0, tiled=True)
    return jnp.sum(got.astype(f32), axis=0), losses


def solution(mesh):
    sections, groups = mesh.devices.shape
    chips = Mesh(mesh.devices.reshape(sections // 2, 2, 4, groups // 4), ALL)
    return jax.shard_map(
        body,
        mesh=chips,
        in_specs=(P(ALL, None), P(ALL, None), P(ALL), P(ALL), P()),
        out_specs=(P(ALL, None), P()),
        check_vma=False,
    )
```

```python
import functools

import jax
import jax.numpy as jnp
from jax import lax
from jax.experimental import pallas as pl
from jax.experimental.pallas import tpu as pltpu
from jax.sharding import Mesh, PartitionSpec as P

SOFTCAP = 30.0
TAIL = 128
ALL = ("x", "core", "y", "z")
VMEM_BYTES = 52 * 1024 * 1024


def shifted(v, axis, by):
    n = lax.axis_size(axis)
    return lax.ppermute(v, axis, [(i, (i + by) % n) for i in range(n)])


def gather(v, axis):
    peers = lax.axis_size(axis)
    return lax.all_to_all(jnp.broadcast_to(v[None], (peers, *v.shape)), axis, 0, 0, tiled=True)


def column_chunk(width):
    return next(c for c in (1152, 128) if width % (2 * c) == 0)


def logits_kernel(n, chunk, where_ref, labels_ref, *refs):
    late = refs[:n]
    early = refs[n : 2 * n]
    own_ref, sib_ref, stats_ref, own_out, sib_out, tok, acc = refs[2 * n :]
    step = pl.program_id(0)
    half = late[0].shape[1]
    rows = late[0].shape[0] // n
    steps = 2 * half // chunk
    vocab = own_ref.shape[0]

    @pl.when(step == 0)
    def _():
        for e in range(n):
            for d in range(n):
                at = pl.multiple_of(where_ref[e * n + d] * rows, rows)
                tok[pl.ds(at, rows), half:] = late[e][d * rows : (d + 1) * rows, :]
                tok[pl.ds(at, rows), :half] = early[d][e * rows : (e + 1) * rows, :]

    def add(u_ref, k):
        columns = tok[:, pl.ds(pl.multiple_of(k * chunk, 128), chunk)]
        part = lax.dot_general(u_ref[...], columns, (((1,), (1,)), ((), ())), preferred_element_type=jnp.float32)

        @pl.when(k == 0)
        def _():
            acc[...] = part

        @pl.when(k > 0)
        def _():
            acc[...] += part

    def finish(base, out, first):
        capped = SOFTCAP * jnp.tanh(acc[...] / SOFTCAP)
        ids = base + lax.broadcasted_iota(jnp.int32, capped.shape, 0)
        hits = ids == labels_ref[...]
        exps = jnp.exp(capped - SOFTCAP)
        total = jnp.sum(exps, axis=0, keepdims=True)
        picked = jnp.sum(jnp.where(hits, capped, 0.0), axis=0, keepdims=True)
        new = jnp.concatenate([total, picked, jnp.zeros((6, total.shape[1]), jnp.float32)], axis=0)
        stats_ref[...] = new if first else stats_ref[...] + new
        terms = exps * (1.0 - (capped / SOFTCAP) ** 2)
        out[...] = terms.T

    @pl.when(step < steps)
    def _():
        add(own_ref, step)

    @pl.when(step == steps - 1)
    def _():
        finish(where_ref[n * n], own_out, True)

    @pl.when(step >= steps)
    def _():
        add(sib_ref, step - steps)

    @pl.when(step == 2 * steps - 1)
    def _():
        finish(where_ref[n * n + 1], sib_out, False)


def logits_and_terms(where, labels, late, early, own, sib):
    n = len(late)
    vocab, width = own.shape
    plane = n * late[0].shape[0]
    chunk = column_chunk(width)
    steps = width // chunk
    whole = lambda a: pl.BlockSpec(a.shape, lambda i: (0, 0))
    terms = jax.ShapeDtypeStruct((plane, vocab), jnp.float32)
    stats = jax.ShapeDtypeStruct((8, plane), jnp.float32)
    return pl.pallas_call(
        functools.partial(logits_kernel, n, chunk),
        grid=(2 * steps,),
        out_shape=(stats, terms, terms),
        in_specs=[pl.BlockSpec(memory_space=pltpu.SMEM), whole(labels)]
        + [whole(a) for a in (*late, *early)]
        + [
            pl.BlockSpec((vocab, chunk), lambda i: (0, jnp.minimum(i, steps - 1))),
            pl.BlockSpec((vocab, chunk), lambda i: (0, jnp.maximum(i - steps, 0))),
        ],
        out_specs=(whole(stats), whole(terms), whole(terms)),
        scratch_shapes=[pltpu.VMEM((plane, width), jnp.bfloat16), pltpu.VMEM((vocab, plane), jnp.float32)],
        compiler_params=pltpu.CompilerParams(vmem_limit_bytes=VMEM_BYTES),
        cost_estimate=pl.CostEstimate(
            flops=4 * plane * vocab * width, bytes_accessed=4 * vocab * width + 4 * plane * width, transcendentals=0
        ),
    )(where, labels, *late, *early, own, sib)


def gradient_kernel(n, where_ref, rows_ref, own_t, sib_t, own_ref, sib_ref, *refs):
    outs = refs[:n]
    own_p, sib_p, columns = refs[n:]
    plane, vocab = own_t.shape
    rows = plane // (n * n)

    @pl.when(pl.program_id(0) == 0)
    def _():
        columns[...] = rows_ref[...].T
        for i in range(n * n):
            at = pl.ds(pl.multiple_of(where_ref[i] * rows, rows), rows)
            to = slice(i * rows, (i + 1) * rows)
            known = columns[at, :]
            fix, scale, labels = known[:, 0:1], known[:, 1:2], known[:, 2:3].astype(jnp.int32)
            for terms, out, base in ((own_t, own_p, where_ref[n * n]), (sib_t, sib_p, where_ref[n * n + 1])):
                ids = base + lax.broadcasted_iota(jnp.int32, (rows, vocab), 1)
                out[to, :] = jnp.where(ids == labels, fix, scale * terms[at, :]).astype(jnp.bfloat16)

    part = jnp.dot(own_p[...], own_ref[...], preferred_element_type=jnp.float32)
    part = part + jnp.dot(sib_p[...], sib_ref[...], preferred_element_type=jnp.float32)
    part = part.astype(jnp.bfloat16)
    for i in range(n):
        outs[i][...] = part[i * n * rows : (i + 1) * n * rows, :]


def gradient_half(n, where, rows, own_t, sib_t, own, sib, second):
    plane, vocab = own_t.shape
    half = own.shape[1] // 2
    chunk = 768 if half % 768 == 0 else 128
    steps = half // chunk
    skip = steps if second else 0
    whole = lambda a: pl.BlockSpec(a.shape, lambda i: (0, 0))
    block = pl.BlockSpec((vocab, chunk), lambda i: (0, i + skip))
    piece = jax.ShapeDtypeStruct((plane // n, half), jnp.bfloat16)
    return pl.pallas_call(
        functools.partial(gradient_kernel, n),
        grid=(steps,),
        out_shape=(piece,) * n,
        in_specs=[pl.BlockSpec(memory_space=pltpu.SMEM), whole(rows), whole(own_t), whole(sib_t), block, block],
        out_specs=(pl.BlockSpec((plane // n, chunk), lambda i: (0, i)),) * n,
        scratch_shapes=[
            pltpu.VMEM((plane, vocab), jnp.bfloat16),
            pltpu.VMEM((plane, vocab), jnp.bfloat16),
            pltpu.VMEM((plane, 8), jnp.float32),
        ],
        compiler_params=pltpu.CompilerParams(vmem_limit_bytes=VMEM_BYTES),
        cost_estimate=pl.CostEstimate(
            flops=4 * plane * vocab * half, bytes_accessed=4 * vocab * half + 2 * plane * half, transcendentals=0
        ),
    )(where, rows, own_t, sib_t, own, sib)


def summed(pieces):
    return sum(p.astype(jnp.float32) for p in pieces).astype(jnp.bfloat16)


def body(hidden, unembed, targets, valid_mask, loss_scale):
    own_rows, width = hidden.shape
    vocab = unembed.shape[0]
    nx, _, ny, nz = (lax.axis_size(a) for a in ALL)
    n = nx
    ix, core, iy, iz = (lax.axis_index(a) for a in ALL)
    plane = nx * ny * nz * own_rows
    per_x = plane // nx
    half = width // 2
    f32, i32 = jnp.float32, jnp.int32

    unembed_sib = lax.ppermute(unembed, "core", [(0, 1), (1, 0)])

    digits = jnp.stack([targets % 256, (targets // 256) % 256, targets // 65536, valid_mask], axis=1)
    tail = jnp.pad(digits, ((0, 0), (0, TAIL - digits.shape[1]))).astype(jnp.bfloat16)
    by_z = gather(jnp.concatenate([hidden, tail], axis=1), "z").reshape(nz * own_rows, width + TAIL)

    tail_own = by_z[:, width:]
    tail_sib = lax.ppermute(tail_own, "core", [(0, 1), (1, 0)])
    first, second = by_z[:, :half], by_z[:, half:width]
    along_x = jnp.concatenate([first] + [shifted(first, "x", e) for e in range(1, n)])
    along_y = jnp.concatenate([second] + [shifted(second, "y", d) for d in range(1, n)])
    early = [along_x] + [shifted(along_x, "y", d) for d in range(1, n)]
    late = [along_y] + [shifted(along_y, "x", e) for e in range(1, n)]

    codes = gather(jnp.stack([tail_own[:, :4], tail_sib[:, :4]]).astype(f32).reshape(1, -1), ("x", "y"))
    codes = codes.reshape(nx * ny, 2, nz * own_rows, 4).astype(i32).transpose(1, 3, 0, 2).reshape(2, 4, plane)
    code = jnp.where(core == 0, codes[1], jnp.roll(codes[1], -per_x, axis=1))
    labels = code[0] + 256 * code[1] + 65536 * code[2]
    weights = code[3].astype(f32)
    counts = jnp.sum((codes[0, 3] + codes[1, 3]).reshape(nx, per_x), axis=1).astype(f32)
    counts_tok = jnp.repeat(jnp.where(core == 0, counts, jnp.roll(counts, -1)), per_x)

    device = lax.axis_index(ALL)
    bases = vocab * jnp.stack([device, device + (1 - 2 * core) * ny * nz])
    near_x, near_y = (ix - jnp.arange(nx)) % nx, (iy - jnp.arange(ny)) % ny
    places = near_x[:, None] * ny + near_y[None, :]
    where_xy = jnp.concatenate([places.ravel(), bases]).astype(i32)
    where_yx = jnp.concatenate([places.T.ravel(), bases]).astype(i32)

    stats, own_t, sib_t = logits_and_terms(where_xy, labels[None], late, early, unembed, unembed_sib)
    stats = gather(stats[:2].reshape(2 * plane // 128, 128), ("x", "y", "z"))
    stats = jnp.sum(stats.reshape(nx * ny * nz, 2 * plane // 128, 128), axis=0)
    total, picked = stats.reshape(2, plane)
    coef = loss_scale * weights / counts_tok
    lse = SOFTCAP + jnp.log(total)
    fix = coef * (jnp.exp(picked - lse) - 1.0) * (1.0 - (picked / SOFTCAP) ** 2)
    rows = jnp.stack([fix, coef / total, labels.astype(f32)] + [jnp.zeros_like(fix)] * 5)

    to_x = gradient_half(n, where_xy, rows, own_t, sib_t, unembed, unembed_sib, True)
    to_y = gradient_half(n, where_yx, rows, own_t, sib_t, unembed, unembed_sib, False)
    got_x = [to_x[0]] + [shifted(to_x[e], "x", -e) for e in range(1, n)]
    got_y = [to_y[0]] + [shifted(to_y[d], "y", -d) for d in range(1, n)]

    sums = jnp.sum((weights * (lse - picked)).reshape(nx, per_x), axis=1)
    sums = jnp.where(core == 0, sums, jnp.roll(sums, 1))
    losses = (sums + lax.ppermute(sums, "core", [(0, 1), (1, 0)])) / counts

    part_x, part_y = summed(got_x), summed(got_y)
    cut = lambda v, i: v[i * nz * own_rows : (i + 1) * nz * own_rows]
    got_y = [cut(part_x, 0)] + [shifted(cut(part_x, d), "y", -d) for d in range(1, n)]
    got_x = [cut(part_y, 0)] + [shifted(cut(part_y, e), "x", -e) for e in range(1, n)]
    part = jnp.concatenate([summed(got_x), summed(got_y)], axis=1).reshape(nz, own_rows, width)
    got = lax.all_to_all(part, "z", 0, 0, tiled=True)
    return jnp.sum(got.astype(f32), axis=0), losses


def solution(mesh):
    sections, groups = mesh.devices.shape
    chips = Mesh(mesh.devices.reshape(sections // 2, 2, 4, groups // 4), ALL)
    return jax.shard_map(
        body,
        mesh=chips,
        in_specs=(P(ALL, None), P(ALL, None), P(ALL), P(ALL), P()),
        out_specs=(P(ALL, None), P()),
        check_vma=False,
    )
```

```python
import functools

import jax
import jax.numpy as jnp
from jax import lax
from jax.experimental import pallas as pl
from jax.experimental.pallas import tpu as pltpu
from jax.sharding import Mesh, PartitionSpec as P

SOFTCAP = 30.0
TAIL = 128
ALL = ("x", "core", "y", "z")
VMEM_BYTES = 52 * 1024 * 1024


def shifted(v, axis, by):
    n = lax.axis_size(axis)
    return lax.ppermute(v, axis, [(i, (i + by) % n) for i in range(n)])


def gather(v, axis):
    peers = lax.axis_size(axis)
    return lax.all_to_all(jnp.broadcast_to(v[None], (peers, *v.shape)), axis, 0, 0, tiled=True)


def column_chunks(width, most):
    chunk = next(c for c in (most, 128) if width % c == 0)
    return [(at, chunk) for at in range(0, width, chunk)]


def fetches(sources, buffers, sems, chunks, offset=0):
    return [
        [
            pltpu.make_async_copy(src.at[:, pl.ds(offset + at, size)], dst.at[:, pl.ds(at, size)], sems.at[j, k])
            for k, (at, size) in enumerate(chunks)
        ]
        for j, (src, dst) in enumerate(zip(sources, buffers))
    ]


def logits_kernel(n, where_ref, *refs):
    late = refs[:n]
    early = refs[n : 2 * n]
    own_ref, sib_ref, sums_ref, own_out, sib_out, own_u, sib_u, tok, acc, sems = refs[2 * n :]
    half = early[0].shape[1]
    rows = late[0].shape[0] // n
    chunks = column_chunks(2 * half, 1536)
    copies = fetches((own_ref, sib_ref), (own_u, sib_u), sems, chunks)
    for part in copies:
        for copy in part:
            copy.start()

    for e in range(n):
        for d in range(n):
            at = pl.multiple_of(where_ref[e * n + d] * rows, rows)
            tok[pl.ds(at, rows), half:] = late[e][d * rows : (d + 1) * rows, :half]
            tok[pl.ds(at, rows), :half] = early[d][e * rows : (e + 1) * rows, :]

    sums = 0.0
    for j, (u, out) in enumerate(((own_u, own_out), (sib_u, sib_out))):
        for k, (at, size) in enumerate(chunks):
            copies[j][k].wait()
            part = lax.dot_general(
                tok[:, at : at + size],
                u[:, at : at + size],
                (((1,), (1,)), ((), ())),
                preferred_element_type=jnp.float32,
            )
            if k:
                part = acc[...] + part
            acc[...] = part
        capped = SOFTCAP * jnp.tanh(acc[...] / SOFTCAP)
        out[...] = capped
        sums = sums + jnp.sum(jnp.exp(capped - SOFTCAP), axis=1, keepdims=True)
    sums_ref[...] = jnp.broadcast_to(sums, sums_ref.shape)


def capped_logits(where, late, early, own, sib):
    n = len(late)
    vocab, width = own.shape
    plane = n * late[0].shape[0]
    vmem, anywhere = pl.BlockSpec(memory_space=pltpu.VMEM), pl.BlockSpec(memory_space=pl.ANY)
    capped = jax.ShapeDtypeStruct((plane, vocab), jnp.float32)
    sums = jax.ShapeDtypeStruct((plane, TAIL), jnp.float32)
    return pl.pallas_call(
        functools.partial(logits_kernel, n),
        out_shape=(sums, capped, capped),
        in_specs=[pl.BlockSpec(memory_space=pltpu.SMEM)] + [vmem] * (2 * n) + [anywhere] * 2,
        out_specs=(vmem,) * 3,
        scratch_shapes=[
            pltpu.VMEM((vocab, width), jnp.bfloat16),
            pltpu.VMEM((vocab, width), jnp.bfloat16),
            pltpu.VMEM((plane, width), jnp.bfloat16),
            pltpu.VMEM((plane, vocab), jnp.float32),
            pltpu.SemaphoreType.DMA((2, len(column_chunks(width, 1536)))),
        ],
        compiler_params=pltpu.CompilerParams(vmem_limit_bytes=VMEM_BYTES),
        cost_estimate=pl.CostEstimate(
            flops=4 * plane * vocab * width, bytes_accessed=4 * vocab * width + 4 * plane * width, transcendentals=0
        ),
    )(where, *late, *early, own, sib)


def labels_kernel(n, where_ref, *refs):
    late = refs[:n]
    tail_ref, sums_ref, own_c, sib_c, rows_ref, own_tail, sib_tail = refs[n:]
    plane, vocab = own_c.shape
    half = late[0].shape[1] - TAIL
    rows = plane // (n * n)
    for e in range(n):
        for d in range(n):
            i = e * n + d
            at = pl.ds(pl.multiple_of(where_ref[i] * rows, rows), rows)
            own_tail[at, :] = late[e][d * rows : (d + 1) * rows, half:].astype(jnp.float32)
            at = pl.ds(pl.multiple_of(where_ref[n * n + 2 + i] * rows, rows), rows)
            sib_tail[at, :] = tail_ref[i * rows : (i + 1) * rows, :].astype(jnp.float32)
    labels = sib_tail[:, 0:1] + 256.0 * sib_tail[:, 1:2] + 65536.0 * sib_tail[:, 2:3]
    picked = 0.0
    for j, capped in enumerate((own_c, sib_c)):
        ids = where_ref[n * n + j] + lax.broadcasted_iota(jnp.int32, (plane, vocab), 1)
        hits = ids == labels.astype(jnp.int32)
        picked = picked + jnp.sum(jnp.where(hits, capped[...], 0.0), axis=1, keepdims=True)
    lane = lax.broadcasted_iota(jnp.int32, (plane, 8), 1)
    columns = jnp.zeros((plane, 8), jnp.float32)
    for i, column in enumerate((sums_ref[:, 0:1], picked, labels, sib_tail[:, 3:4], own_tail[:, 3:4])):
        columns = jnp.where(lane == i, column, columns)
    rows_ref[...] = columns.T


def labels_and_sums(where, late, tail, sums, own_c, sib_c):
    n = len(late)
    plane = own_c.shape[0]
    vmem = pl.BlockSpec(memory_space=pltpu.VMEM)
    return pl.pallas_call(
        functools.partial(labels_kernel, n),
        out_shape=jax.ShapeDtypeStruct((8, plane), jnp.float32),
        in_specs=[pl.BlockSpec(memory_space=pltpu.SMEM)] + [vmem] * (n + 4),
        out_specs=vmem,
        scratch_shapes=[pltpu.VMEM((plane, TAIL), jnp.float32)] * 2,
        compiler_params=pltpu.CompilerParams(vmem_limit_bytes=16 * 1024 * 1024),
    )(where, *late, tail, sums, own_c, sib_c)


def gradient_kernel(n, where_ref, rows_ref, own_c, sib_c, own_ref, sib_ref, *refs):
    outs = refs[:n]
    own_p, sib_p, columns = refs[n:]
    plane, vocab = own_c.shape
    rows = plane // (n * n)

    @pl.when(pl.program_id(0) == 0)
    def _():
        columns[...] = rows_ref[...].T
        for i in range(n * n):
            at = pl.ds(pl.multiple_of(where_ref[i] * rows, rows), rows)
            to = slice(i * rows, (i + 1) * rows)
            known = columns[at, :]
            lse, coef, labels = known[:, 0:1], known[:, 1:2], known[:, 2:3].astype(jnp.int32)
            for c_ref, out, base in ((own_c, own_p, where_ref[n * n]), (sib_c, sib_p, where_ref[n * n + 1])):
                capped = c_ref[at, :]
                ids = base + lax.broadcasted_iota(jnp.int32, (rows, vocab), 1)
                grad = jnp.exp(capped - lse) - jnp.where(ids == labels, 1.0, 0.0)
                out[to, :] = (coef * grad * (1.0 - (capped / SOFTCAP) ** 2)).astype(jnp.bfloat16)

    part = jnp.dot(own_p[...], own_ref[...], preferred_element_type=jnp.float32)
    part = part + jnp.dot(sib_p[...], sib_ref[...], preferred_element_type=jnp.float32)
    part = part.astype(jnp.bfloat16)
    for i in range(n):
        outs[i][...] = part[i * n * rows : (i + 1) * n * rows, :]


def gradient_half(n, where, rows, own_c, sib_c, own, sib, second):
    plane, vocab = own_c.shape
    half = own.shape[1] // 2
    chunk = 1152 if half % 1152 == 0 else 128
    steps = half // chunk
    skip = steps if second else 0
    whole = lambda a: pl.BlockSpec(a.shape, lambda i: (0, 0))
    block = pl.BlockSpec((vocab, chunk), lambda i: (0, i + skip))
    piece = jax.ShapeDtypeStruct((plane // n, half), jnp.bfloat16)
    return pl.pallas_call(
        functools.partial(gradient_kernel, n),
        grid=(steps,),
        out_shape=(piece,) * n,
        in_specs=[pl.BlockSpec(memory_space=pltpu.SMEM), whole(rows), whole(own_c), whole(sib_c), block, block],
        out_specs=(pl.BlockSpec((plane // n, chunk), lambda i: (0, i)),) * n,
        scratch_shapes=[
            pltpu.VMEM((plane, vocab), jnp.bfloat16),
            pltpu.VMEM((plane, vocab), jnp.bfloat16),
            pltpu.VMEM((plane, 8), jnp.float32),
        ],
        compiler_params=pltpu.CompilerParams(vmem_limit_bytes=VMEM_BYTES),
        cost_estimate=pl.CostEstimate(
            flops=4 * plane * vocab * half, bytes_accessed=4 * vocab * half + 2 * plane * half, transcendentals=0
        ),
    )(where, rows, own_c, sib_c, own, sib)


def summed(pieces):
    return sum(p.astype(jnp.float32) for p in pieces).astype(jnp.bfloat16)


def body(hidden, unembed, targets, valid_mask, loss_scale):
    own_rows, width = hidden.shape
    vocab = unembed.shape[0]
    nx, _, ny, nz = (lax.axis_size(a) for a in ALL)
    n = nx
    ix, core, iy, iz = (lax.axis_index(a) for a in ALL)
    plane = nx * ny * nz * own_rows
    per_x = plane // nx
    half = width // 2
    f32, i32 = jnp.float32, jnp.int32

    unembed_sib = lax.ppermute(unembed, "core", [(0, 1), (1, 0)])

    digits = jnp.stack([targets % 256, (targets // 256) % 256, targets // 65536, valid_mask], axis=1)
    tail = jnp.pad(digits, ((0, 0), (0, TAIL - digits.shape[1]))).astype(jnp.bfloat16)
    by_z = gather(jnp.concatenate([hidden, tail], axis=1), "z").reshape(nz * own_rows, width + TAIL)

    by_z, unembed_sib = lax.optimization_barrier((by_z, unembed_sib))

    first, second = by_z[:, :half], by_z[:, half:]
    along_x = jnp.concatenate([first] + [shifted(first, "x", e) for e in range(1, n)])
    along_y = jnp.concatenate([second] + [shifted(second, "y", d) for d in range(1, n)])
    along_x, along_y = lax.optimization_barrier((along_x, along_y))
    late = [along_y] + [shifted(along_y, "x", e) for e in range(1, n)]
    early = [along_x] + [shifted(along_x, "y", d) for d in range(1, n)]
    tail_sib = lax.ppermute(jnp.concatenate([v[:, half:] for v in late]), "core", [(0, 1), (1, 0)])

    device = lax.axis_index(ALL)
    bases = vocab * jnp.stack([device, device + (1 - 2 * core) * ny * nz])
    near_x, near_y = (ix - jnp.arange(nx)) % nx, (iy - jnp.arange(ny)) % ny
    places = near_x[:, None] * ny + near_y[None, :]
    label_places = ((near_x - core) % nx)[:, None] * ny + near_y[None, :]
    where_xy = jnp.concatenate([places.ravel(), bases, label_places.ravel()]).astype(i32)
    where_yx = jnp.concatenate([places.T.ravel(), bases]).astype(i32)

    sums, own_c, sib_c = capped_logits(where_xy, late, early, unembed, unembed_sib)
    known = labels_and_sums(where_xy, late, tail_sib, sums, own_c, sib_c)
    stats = gather(known[:2].reshape(2 * plane // 128, 128), ("x", "y", "z"))
    labels, weights = known[2], known[3]
    by_x = lambda v: jnp.sum(v.reshape(nx, per_x), axis=1)
    of_tokens = by_x(weights)
    counts = by_x(known[4]) + jnp.where(core == 0, of_tokens, jnp.roll(of_tokens, 1))
    counts_tok = jnp.repeat(jnp.where(core == 0, counts, jnp.roll(counts, -1)), per_x)
    coef = loss_scale * weights / counts_tok
    stats = jnp.sum(stats.reshape(nx * ny * nz, 2 * plane // 128, 128), axis=0)
    total, picked = stats.reshape(2, plane)
    lse = SOFTCAP + jnp.log(total)
    rows = jnp.stack([lse, coef, labels] + [jnp.zeros_like(lse)] * 5)

    to_x = gradient_half(n, where_xy, rows, own_c, sib_c, unembed, unembed_sib, True)
    to_y = gradient_half(n, where_yx, rows, own_c, sib_c, unembed, unembed_sib, False)
    got_x = [to_x[0]] + [shifted(to_x[e], "x", -e) for e in range(1, n)]
    got_y = [to_y[0]] + [shifted(to_y[d], "y", -d) for d in range(1, n)]

    sums = jnp.sum((weights * (lse - picked)).reshape(nx, per_x), axis=1)
    sums = jnp.where(core == 0, sums, jnp.roll(sums, 1))
    losses = (sums + lax.ppermute(sums, "core", [(0, 1), (1, 0)])) / counts

    part_x, part_y = summed(got_x), summed(got_y)
    cut = lambda v, i: v[i * nz * own_rows : (i + 1) * nz * own_rows]
    got_y = [cut(part_x, 0)] + [shifted(cut(part_x, d), "y", -d) for d in range(1, n)]
    got_x = [cut(part_y, 0)] + [shifted(cut(part_y, e), "x", -e) for e in range(1, n)]
    part = jnp.concatenate([summed(got_x), summed(got_y)], axis=1).reshape(nz, own_rows, width)
    got = lax.all_to_all(part, "z", 0, 0, tiled=True)
    return jnp.sum(got.astype(f32), axis=0), losses


def solution(mesh):
    sections, groups = mesh.devices.shape
    chips = Mesh(mesh.devices.reshape(sections // 2, 2, 4, groups // 4), ALL)
    return jax.shard_map(
        body,
        mesh=chips,
        in_specs=(P(ALL, None), P(ALL, None), P(ALL), P(ALL), P()),
        out_specs=(P(ALL, None), P()),
        check_vma=False,
    )
```

```python
import functools

import jax
import jax.numpy as jnp
from jax import lax
from jax.experimental import pallas as pl
from jax.experimental.pallas import tpu as pltpu
from jax.sharding import Mesh, PartitionSpec as P

SOFTCAP = 30.0
TAIL = 128
ALL = ("x", "core", "y", "z")
VMEM_BYTES = 52 * 1024 * 1024


def shifted(v, axis, by):
    n = lax.axis_size(axis)
    return lax.ppermute(v, axis, [(i, (i + by) % n) for i in range(n)])


def gather(v, axis):
    peers = lax.axis_size(axis)
    return lax.all_to_all(jnp.broadcast_to(v[None], (peers, *v.shape)), axis, 0, 0, tiled=True)


def column_chunks(width, most):
    chunk = next(c for c in (most, 128) if width % c == 0)
    return [(at, chunk) for at in range(0, width, chunk)]


def fetches(sources, buffers, sems, chunks, offset=0):
    return [
        [
            pltpu.make_async_copy(src.at[:, pl.ds(offset + at, size)], dst.at[:, pl.ds(at, size)], sems.at[j, k])
            for k, (at, size) in enumerate(chunks)
        ]
        for j, (src, dst) in enumerate(zip(sources, buffers))
    ]


def logits_kernel(n, where_ref, *refs):
    late = refs[:n]
    early = refs[n : 2 * n]
    own_ref, sib_ref, sums_ref, own_out, sib_out, own_u, sib_u, tok, acc, sems = refs[2 * n :]
    half = early[0].shape[1]
    rows = late[0].shape[0] // n
    chunks = column_chunks(2 * half, 1536)
    copies = fetches((own_ref, sib_ref), (own_u, sib_u), sems, chunks)
    for part in copies:
        for copy in part:
            copy.start()

    for e in range(n):
        for d in range(n):
            at = pl.multiple_of(where_ref[e * n + d] * rows, rows)
            tok[pl.ds(at, rows), half:] = late[e][d * rows : (d + 1) * rows, :half]
            tok[pl.ds(at, rows), :half] = early[d][e * rows : (e + 1) * rows, :]

    sums = 0.0
    for j, (u, out) in enumerate(((own_u, own_out), (sib_u, sib_out))):
        for k, (at, size) in enumerate(chunks):
            copies[j][k].wait()
            part = lax.dot_general(
                tok[:, at : at + size],
                u[:, at : at + size],
                (((1,), (1,)), ((), ())),
                preferred_element_type=jnp.float32,
            )
            if k:
                part = acc[...] + part
            acc[...] = part
        capped = SOFTCAP * jnp.tanh(acc[...] / SOFTCAP)
        out[...] = capped
        sums = sums + jnp.sum(jnp.exp(capped - SOFTCAP), axis=1, keepdims=True)
    sums_ref[...] = jnp.broadcast_to(sums, sums_ref.shape)


def capped_logits(where, late, early, own, sib):
    n = len(late)
    vocab, width = own.shape
    plane = n * late[0].shape[0]
    vmem, hbm = pl.BlockSpec(memory_space=pltpu.VMEM), pl.BlockSpec(memory_space=pltpu.HBM)
    capped = jax.ShapeDtypeStruct((plane, vocab), jnp.float32)
    sums = jax.ShapeDtypeStruct((plane, TAIL), jnp.float32)
    return pl.pallas_call(
        functools.partial(logits_kernel, n),
        out_shape=(sums, capped, capped),
        in_specs=[pl.BlockSpec(memory_space=pltpu.SMEM)] + [vmem] * (2 * n) + [hbm] * 2,
        out_specs=(vmem,) * 3,
        scratch_shapes=[
            pltpu.VMEM((vocab, width), jnp.bfloat16),
            pltpu.VMEM((vocab, width), jnp.bfloat16),
            pltpu.VMEM((plane, width), jnp.bfloat16),
            pltpu.VMEM((plane, vocab), jnp.float32),
            pltpu.SemaphoreType.DMA((2, len(column_chunks(width, 1536)))),
        ],
        compiler_params=pltpu.CompilerParams(vmem_limit_bytes=VMEM_BYTES),
        cost_estimate=pl.CostEstimate(
            flops=4 * plane * vocab * width, bytes_accessed=4 * vocab * width + 4 * plane * width, transcendentals=0
        ),
    )(where, *late, *early, own, sib)


def labels_kernel(n, where_ref, own_ref, sib_ref, sums_ref, own_c, sib_c, rows_ref, own_tail, sib_tail):
    plane, vocab = own_c.shape
    rows = plane // (n * n)
    for i in range(n * n):
        here = slice(i * rows, (i + 1) * rows)
        own_tail[pl.ds(pl.multiple_of(where_ref[i] * rows, rows), rows), :] = own_ref[here, :].astype(jnp.float32)
        at = pl.ds(pl.multiple_of(where_ref[n * n + 2 + i] * rows, rows), rows)
        sib_tail[at, :] = sib_ref[here, :].astype(jnp.float32)
    labels = sib_tail[:, 0:1] + 256.0 * sib_tail[:, 1:2] + 65536.0 * sib_tail[:, 2:3]
    picked = 0.0
    for j, capped in enumerate((own_c, sib_c)):
        ids = where_ref[n * n + j] + lax.broadcasted_iota(jnp.int32, (plane, vocab), 1)
        hits = ids == labels.astype(jnp.int32)
        picked = picked + jnp.sum(jnp.where(hits, capped[...], 0.0), axis=1, keepdims=True)
    lane = lax.broadcasted_iota(jnp.int32, (plane, 8), 1)
    columns = jnp.zeros((plane, 8), jnp.float32)
    for i, column in enumerate((sums_ref[:, 0:1], picked, labels, sib_tail[:, 3:4], own_tail[:, 3:4])):
        columns = jnp.where(lane == i, column, columns)
    rows_ref[...] = columns.T


def labels_and_sums(n, where, own_tail, sib_tail, sums, own_c, sib_c):
    plane = own_c.shape[0]
    vmem = pl.BlockSpec(memory_space=pltpu.VMEM)
    return pl.pallas_call(
        functools.partial(labels_kernel, n),
        out_shape=jax.ShapeDtypeStruct((8, plane), jnp.float32),
        in_specs=[pl.BlockSpec(memory_space=pltpu.SMEM)] + [vmem] * 5,
        out_specs=vmem,
        scratch_shapes=[pltpu.VMEM((plane, TAIL), jnp.float32)] * 2,
        compiler_params=pltpu.CompilerParams(vmem_limit_bytes=8 * 1024 * 1024),
    )(where, own_tail, sib_tail, sums, own_c, sib_c)


def gradient_kernel(n, where_ref, rows_ref, own_c, sib_c, own_ref, sib_ref, *refs):
    outs = refs[:n]
    own_p, sib_p, columns = refs[n:]
    plane, vocab = own_c.shape
    rows = plane // (n * n)

    @pl.when(pl.program_id(0) == 0)
    def _():
        columns[...] = rows_ref[...].T
        for i in range(n * n):
            at = pl.ds(pl.multiple_of(where_ref[i] * rows, rows), rows)
            to = slice(i * rows, (i + 1) * rows)
            known = columns[at, :]
            lse, coef, labels = known[:, 0:1], known[:, 1:2], known[:, 2:3].astype(jnp.int32)
            for c_ref, out, base in ((own_c, own_p, where_ref[n * n]), (sib_c, sib_p, where_ref[n * n + 1])):
                capped = c_ref[at, :]
                ids = base + lax.broadcasted_iota(jnp.int32, (rows, vocab), 1)
                grad = jnp.exp(capped - lse) - jnp.where(ids == labels, 1.0, 0.0)
                out[to, :] = (coef * grad * (1.0 - (capped / SOFTCAP) ** 2)).astype(jnp.bfloat16)

    part = jnp.dot(own_p[...], own_ref[...], preferred_element_type=jnp.float32)
    part = part + jnp.dot(sib_p[...], sib_ref[...], preferred_element_type=jnp.float32)
    part = part.astype(jnp.bfloat16)
    for i in range(n):
        outs[i][...] = part[i * n * rows : (i + 1) * n * rows, :]


def gradient_part(n, where, rows, own_c, sib_c, own, sib, start, size):
    plane, vocab = own_c.shape
    chunk = next(c for c in range(1152, 0, -128) if size % c == 0 and start % c == 0)
    steps, skip = size // chunk, start // chunk
    whole = lambda a: pl.BlockSpec(a.shape, lambda i: (0, 0))
    block = pl.BlockSpec((vocab, chunk), lambda i: (0, i + skip))
    piece = jax.ShapeDtypeStruct((plane // n, size), jnp.bfloat16)
    return pl.pallas_call(
        functools.partial(gradient_kernel, n),
        grid=(steps,),
        out_shape=(piece,) * n,
        in_specs=[pl.BlockSpec(memory_space=pltpu.SMEM), whole(rows), whole(own_c), whole(sib_c), block, block],
        out_specs=(pl.BlockSpec((plane // n, chunk), lambda i: (0, i)),) * n,
        scratch_shapes=[
            pltpu.VMEM((plane, vocab), jnp.bfloat16),
            pltpu.VMEM((plane, vocab), jnp.bfloat16),
            pltpu.VMEM((plane, 8), jnp.float32),
        ],
        compiler_params=pltpu.CompilerParams(vmem_limit_bytes=VMEM_BYTES),
        cost_estimate=pl.CostEstimate(
            flops=4 * plane * vocab * size, bytes_accessed=4 * vocab * size + 2 * plane * size, transcendentals=0
        ),
    )(where, rows, own_c, sib_c, own, sib)


def summed(pieces):
    return sum(p.astype(jnp.float32) for p in pieces).astype(jnp.bfloat16)


def body(hidden, unembed, targets, valid_mask, loss_scale):
    own_rows, width = hidden.shape
    vocab = unembed.shape[0]
    nx, _, ny, nz = (lax.axis_size(a) for a in ALL)
    n = nx
    ix, core, iy, iz = (lax.axis_index(a) for a in ALL)
    plane = nx * ny * nz * own_rows
    per_x = plane // nx
    half = width // 2
    f32, i32 = jnp.float32, jnp.int32

    unembed_sib = lax.ppermute(unembed, "core", [(0, 1), (1, 0)])

    digits = jnp.stack([targets % 256, (targets // 256) % 256, targets // 65536, valid_mask], axis=1)
    tail = jnp.pad(digits, ((0, 0), (0, TAIL - digits.shape[1]))).astype(jnp.bfloat16)
    by_z = gather(jnp.concatenate([hidden, tail], axis=1), "z").reshape(nz * own_rows, width + TAIL)

    by_z, unembed_sib = lax.optimization_barrier((by_z, unembed_sib))

    first, second = by_z[:, :half], by_z[:, half:]
    along_x = jnp.concatenate([first] + [shifted(first, "x", e) for e in range(1, n)])
    along_y = jnp.concatenate([second] + [shifted(second, "y", d) for d in range(1, n)])
    along_x, along_y = lax.optimization_barrier((along_x, along_y))
    late = [along_y] + [shifted(along_y, "x", e) for e in range(1, n)]
    early = [along_x] + [shifted(along_x, "y", d) for d in range(1, n)]
    tail_own = jnp.concatenate([v[:, half:] for v in late])
    tail_sib = lax.ppermute(tail_own, "core", [(0, 1), (1, 0)])

    device = lax.axis_index(ALL)
    bases = vocab * jnp.stack([device, device + (1 - 2 * core) * ny * nz])
    near_x, near_y = (ix - jnp.arange(nx)) % nx, (iy - jnp.arange(ny)) % ny
    places = near_x[:, None] * ny + near_y[None, :]
    label_places = ((near_x - core) % nx)[:, None] * ny + near_y[None, :]
    where_xy = jnp.concatenate([places.ravel(), bases, label_places.ravel()]).astype(i32)
    where_yx = jnp.concatenate([places.T.ravel(), bases]).astype(i32)

    sums, own_c, sib_c = capped_logits(where_xy, late, early, unembed, unembed_sib)
    known = labels_and_sums(n, where_xy, tail_own, tail_sib, sums, own_c, sib_c)
    stats = gather(known[:2].reshape(2 * plane // 128, 128), ("x", "y", "z"))
    labels, weights = known[2], known[3]
    by_x = lambda v: jnp.sum(v.reshape(nx, per_x), axis=1)
    of_tokens = by_x(weights)
    counts = by_x(known[4]) + jnp.where(core == 0, of_tokens, jnp.roll(of_tokens, 1))
    counts_tok = jnp.repeat(jnp.where(core == 0, counts, jnp.roll(counts, -1)), per_x)
    coef = loss_scale * weights / counts_tok
    stats = jnp.sum(stats.reshape(nx * ny * nz, 2 * plane // 128, 128), axis=0)
    total, picked = stats.reshape(2, plane)
    lse = SOFTCAP + jnp.log(total)
    rows = jnp.stack([lse, coef, labels] + [jnp.zeros_like(lse)] * 5)

    split = half
    to_x = gradient_part(n, where_xy, rows, own_c, sib_c, unembed, unembed_sib, 0, split)
    to_y = gradient_part(n, where_yx, rows, own_c, sib_c, unembed, unembed_sib, split, width - split)
    to_y, lse, picked = lax.optimization_barrier((to_y, lse, picked))
    got_x = [to_x[0]] + [shifted(to_x[e], "x", -e) for e in range(1, n)]
    got_y = [to_y[0]] + [shifted(to_y[d], "y", -d) for d in range(1, n)]

    sums = by_x(weights * (lse - picked))
    sums = jnp.where(core == 0, sums, jnp.roll(sums, 1))
    losses = (sums + lax.ppermute(sums, "core", [(0, 1), (1, 0)])) / counts

    part_x, part_y = summed(got_x), summed(got_y)
    cut = lambda v, i: v[i * nz * own_rows : (i + 1) * nz * own_rows]
    got_y = [cut(part_x, 0)] + [shifted(cut(part_x, d), "y", -d) for d in range(1, n)]
    got_x = [cut(part_y, 0)] + [shifted(cut(part_y, e), "x", -e) for e in range(1, n)]
    part = jnp.concatenate([summed(got_y), summed(got_x)], axis=1).reshape(nz, own_rows, width)
    got = lax.all_to_all(part, "z", 0, 0, tiled=True)
    return jnp.sum(got.astype(f32), axis=0), losses


def solution(mesh):
    sections, groups = mesh.devices.shape
    chips = Mesh(mesh.devices.reshape(sections // 2, 2, 4, groups // 4), ALL)
    return jax.shard_map(
        body,
        mesh=chips,
        in_specs=(P(ALL, None), P(ALL, None), P(ALL), P(ALL), P()),
        out_specs=(P(ALL, None), P()),
        check_vma=False,
    )
```

```python
import functools

import jax
import jax.numpy as jnp
from jax import lax
from jax.experimental import pallas as pl
from jax.experimental.pallas import tpu as pltpu
from jax.sharding import Mesh, PartitionSpec as P

SOFTCAP = 30.0
TAIL = 128
ALL = ("x", "core", "y", "z")
VMEM_BYTES = 52 * 1024 * 1024


def shifted(v, axis, by):
    n = lax.axis_size(axis)
    return lax.ppermute(v, axis, [(i, (i + by) % n) for i in range(n)])


def column_chunks(width, most):
    chunk = next(c for c in (most, 128) if width % c == 0)
    return [(at, chunk) for at in range(0, width, chunk)]


def fetches(sources, buffers, sems, chunks, offset=0):
    return [
        [
            pltpu.make_async_copy(src.at[:, pl.ds(offset + at, size)], dst.at[:, pl.ds(at, size)], sems.at[j, k])
            for k, (at, size) in enumerate(chunks)
        ]
        for j, (src, dst) in enumerate(zip(sources, buffers))
    ]


def logits_kernel(n, where_ref, *refs):
    late = refs[:n]
    early = refs[n : 2 * n]
    own_ref, sib_ref, sums_ref, own_out, sib_out, own_u, sib_u, tok, acc, sems = refs[2 * n :]
    half = early[0].shape[1]
    rows = late[0].shape[0] // n
    chunks = column_chunks(2 * half, 1536)
    copies = fetches((own_ref, sib_ref), (own_u, sib_u), sems, chunks)
    for part in copies:
        for copy in part:
            copy.start()

    for e in range(n):
        for d in range(n):
            at = pl.multiple_of(where_ref[e * n + d] * rows, rows)
            tok[pl.ds(at, rows), half:] = late[e][d * rows : (d + 1) * rows, :half]
            tok[pl.ds(at, rows), :half] = early[d][e * rows : (e + 1) * rows, :]

    sums = 0.0
    for j, (u, out) in enumerate(((own_u, own_out), (sib_u, sib_out))):
        for k, (at, size) in enumerate(chunks):
            copies[j][k].wait()
            part = lax.dot_general(
                tok[:, at : at + size],
                u[:, at : at + size],
                (((1,), (1,)), ((), ())),
                preferred_element_type=jnp.float32,
            )
            if k:
                part = acc[...] + part
            acc[...] = part
        capped = SOFTCAP * jnp.tanh(acc[...] / SOFTCAP)
        out[...] = capped
        sums = sums + jnp.sum(jnp.exp(capped - SOFTCAP), axis=1, keepdims=True)
    sums_ref[...] = jnp.broadcast_to(sums, sums_ref.shape)


def capped_logits(where, late, early, own, sib):
    n = len(late)
    vocab, width = own.shape
    plane = n * late[0].shape[0]
    vmem, hbm = pl.BlockSpec(memory_space=pltpu.VMEM), pl.BlockSpec(memory_space=pltpu.HBM)
    capped = jax.ShapeDtypeStruct((plane, vocab), jnp.float32)
    sums = jax.ShapeDtypeStruct((plane, TAIL), jnp.float32)
    return pl.pallas_call(
        functools.partial(logits_kernel, n),
        out_shape=(sums, capped, capped),
        in_specs=[pl.BlockSpec(memory_space=pltpu.SMEM)] + [vmem] * (2 * n) + [hbm] * 2,
        out_specs=(vmem,) * 3,
        scratch_shapes=[
            pltpu.VMEM((vocab, width), jnp.bfloat16),
            pltpu.VMEM((vocab, width), jnp.bfloat16),
            pltpu.VMEM((plane, width), jnp.bfloat16),
            pltpu.VMEM((plane, vocab), jnp.float32),
            pltpu.SemaphoreType.DMA((2, len(column_chunks(width, 1536)))),
        ],
        compiler_params=pltpu.CompilerParams(vmem_limit_bytes=VMEM_BYTES),
        cost_estimate=pl.CostEstimate(
            flops=4 * plane * vocab * width, bytes_accessed=4 * vocab * width + 4 * plane * width, transcendentals=0
        ),
    )(where, *late, *early, own, sib)


def labels_kernel(n, where_ref, own_ref, sib_ref, sums_ref, own_c, sib_c, rows_ref, send_ref, own_tail, sib_tail):
    plane, vocab = own_c.shape
    rows = plane // (n * n)
    for i in range(n * n):
        here = slice(i * rows, (i + 1) * rows)
        own_tail[pl.ds(pl.multiple_of(where_ref[i] * rows, rows), rows), :] = own_ref[here, :].astype(jnp.float32)
        at = pl.ds(pl.multiple_of(where_ref[n * n + 2 + i] * rows, rows), rows)
        sib_tail[at, :] = sib_ref[here, :].astype(jnp.float32)
    labels = sib_tail[:, 0:1] + 256.0 * sib_tail[:, 1:2] + 65536.0 * sib_tail[:, 2:3]
    picked = 0.0
    for j, capped in enumerate((own_c, sib_c)):
        ids = where_ref[n * n + j] + lax.broadcasted_iota(jnp.int32, (plane, vocab), 1)
        hits = ids == labels.astype(jnp.int32)
        picked = picked + jnp.sum(jnp.where(hits, capped[...], 0.0), axis=1, keepdims=True)
    lane = lax.broadcasted_iota(jnp.int32, (plane, 8), 1)
    columns = jnp.zeros((plane, 8), jnp.float32)
    for i, column in enumerate((sums_ref[:, 0:1], picked, labels, sib_tail[:, 3:4], own_tail[:, 3:4])):
        columns = jnp.where(lane == i, column, columns)
    known = columns.T
    rows_ref[...] = known
    lanes = send_ref.shape[1]
    one = [known[i : i + 1, at : at + lanes] for i in range(2) for at in range(0, plane, lanes)]
    block = jnp.concatenate(one * (8 // len(one)), axis=0)
    for i in range(send_ref.shape[0] // 8):
        send_ref[i * 8 : (i + 1) * 8, :] = block


def labels_and_sums(n, peers, where, own_tail, sib_tail, sums, own_c, sib_c):
    plane = own_c.shape[0]
    vmem = pl.BlockSpec(memory_space=pltpu.VMEM)
    return pl.pallas_call(
        functools.partial(labels_kernel, n),
        out_shape=(
            jax.ShapeDtypeStruct((8, plane), jnp.float32),
            jax.ShapeDtypeStruct((peers * 2 * plane // 128, 128), jnp.float32),
        ),
        in_specs=[pl.BlockSpec(memory_space=pltpu.SMEM)] + [vmem] * 5,
        out_specs=(vmem, vmem),
        scratch_shapes=[pltpu.VMEM((plane, TAIL), jnp.float32)] * 2,
        compiler_params=pltpu.CompilerParams(vmem_limit_bytes=8 * 1024 * 1024),
    )(where, own_tail, sib_tail, sums, own_c, sib_c)


def gradient_kernel(n, where_ref, rows_ref, own_c, sib_c, own_ref, sib_ref, *refs):
    outs = refs[:n]
    own_p, sib_p, columns = refs[n:]
    plane, vocab = own_c.shape
    rows = plane // (n * n)

    @pl.when(pl.program_id(0) == 0)
    def _():
        columns[...] = rows_ref[...].T
        for i in range(n * n):
            at = pl.ds(pl.multiple_of(where_ref[i] * rows, rows), rows)
            to = slice(i * rows, (i + 1) * rows)
            known = columns[at, :]
            lse, coef, labels = known[:, 0:1], known[:, 1:2], known[:, 2:3].astype(jnp.int32)
            for c_ref, out, base in ((own_c, own_p, where_ref[n * n]), (sib_c, sib_p, where_ref[n * n + 1])):
                capped = c_ref[at, :]
                ids = base + lax.broadcasted_iota(jnp.int32, (rows, vocab), 1)
                grad = jnp.exp(capped - lse) - jnp.where(ids == labels, 1.0, 0.0)
                out[to, :] = (coef * grad * (1.0 - (capped / SOFTCAP) ** 2)).astype(jnp.bfloat16)

    part = jnp.dot(own_p[...], own_ref[...], preferred_element_type=jnp.float32)
    part = part + jnp.dot(sib_p[...], sib_ref[...], preferred_element_type=jnp.float32)
    part = part.astype(jnp.bfloat16)
    for i in range(n):
        outs[i][...] = part[i * n * rows : (i + 1) * n * rows, :]


def gradient_part(n, where, rows, own_c, sib_c, own, sib, start, size):
    plane, vocab = own_c.shape
    chunk = next(c for c in range(1152, 0, -128) if size % c == 0 and start % c == 0)
    steps, skip = size // chunk, start // chunk
    whole = lambda a: pl.BlockSpec(a.shape, lambda i: (0, 0))
    block = pl.BlockSpec((vocab, chunk), lambda i: (0, i + skip))
    piece = jax.ShapeDtypeStruct((plane // n, size), jnp.bfloat16)
    return pl.pallas_call(
        functools.partial(gradient_kernel, n),
        grid=(steps,),
        out_shape=(piece,) * n,
        in_specs=[pl.BlockSpec(memory_space=pltpu.SMEM), whole(rows), whole(own_c), whole(sib_c), block, block],
        out_specs=(pl.BlockSpec((plane // n, chunk), lambda i: (0, i)),) * n,
        scratch_shapes=[
            pltpu.VMEM((plane, vocab), jnp.bfloat16),
            pltpu.VMEM((plane, vocab), jnp.bfloat16),
            pltpu.VMEM((plane, 8), jnp.float32),
        ],
        compiler_params=pltpu.CompilerParams(vmem_limit_bytes=VMEM_BYTES),
        cost_estimate=pl.CostEstimate(
            flops=4 * plane * vocab * size, bytes_accessed=4 * vocab * size + 2 * plane * size, transcendentals=0
        ),
    )(where, rows, own_c, sib_c, own, sib)


def summed(pieces):
    return sum(p.astype(jnp.float32) for p in pieces).astype(jnp.bfloat16)


def body(hidden, unembed, targets, valid_mask, loss_scale):
    own_rows, width = hidden.shape
    vocab = unembed.shape[0]
    nx, _, ny, nz = (lax.axis_size(a) for a in ALL)
    n = nx
    ix, core, iy, iz = (lax.axis_index(a) for a in ALL)
    plane = nx * ny * nz * own_rows
    per_x = plane // nx
    half = width // 2
    f32, i32 = jnp.float32, jnp.int32

    unembed_sib = lax.ppermute(unembed, "core", [(0, 1), (1, 0)])

    digits = jnp.stack([targets % 256, (targets // 256) % 256, targets // 65536, valid_mask], axis=1)
    tail = jnp.pad(digits, ((0, 0), (0, TAIL - digits.shape[1]))).astype(jnp.bfloat16)
    for_all = lambda v: jnp.broadcast_to(v[None], (nz, *v.shape))
    mine = jnp.concatenate([for_all(hidden), for_all(tail)], axis=2)
    by_z = lax.all_to_all(mine, "z", 0, 0, tiled=True).reshape(nz * own_rows, width + TAIL)
    by_z, unembed_sib = lax.optimization_barrier((by_z, unembed_sib))

    first, second = by_z[:, :half], by_z[:, half:]
    along_x = jnp.concatenate([first] + [shifted(first, "x", e) for e in range(1, n)])
    along_y = jnp.concatenate([second] + [shifted(second, "y", d) for d in range(1, n)])
    along_x, along_y = lax.optimization_barrier((along_x, along_y))
    late = [along_y] + [shifted(along_y, "x", e) for e in range(1, n)]
    early = [along_x] + [shifted(along_x, "y", d) for d in range(1, n)]
    tail_own = jnp.concatenate([v[:, half:] for v in late])
    tail_sib = lax.ppermute(tail_own, "core", [(0, 1), (1, 0)])

    device = lax.axis_index(ALL)
    bases = vocab * jnp.stack([device, device + (1 - 2 * core) * ny * nz])
    near_x, near_y = (ix - jnp.arange(nx)) % nx, (iy - jnp.arange(ny)) % ny
    places = near_x[:, None] * ny + near_y[None, :]
    label_places = ((near_x - core) % nx)[:, None] * ny + near_y[None, :]
    where_xy = jnp.concatenate([places.ravel(), bases, label_places.ravel()]).astype(i32)
    where_yx = jnp.concatenate([places.T.ravel(), bases]).astype(i32)

    sums, own_c, sib_c = capped_logits(where_xy, late, early, unembed, unembed_sib)
    peers, lines = nx * ny * nz, 2 * plane // 128
    known, send = labels_and_sums(n, peers, where_xy, tail_own, tail_sib, sums, own_c, sib_c)
    stats = lax.all_to_all(send.reshape(peers, lines, 128), ("x", "y", "z"), 0, 0, tiled=True)
    labels, weights = known[2], known[3]
    by_x = lambda v: jnp.sum(v.reshape(nx, per_x), axis=1)
    of_tokens = by_x(weights)
    counts = by_x(known[4]) + jnp.where(core == 0, of_tokens, jnp.roll(of_tokens, 1))
    counts_tok = jnp.repeat(jnp.where(core == 0, counts, jnp.roll(counts, -1)), per_x)
    coef = loss_scale * weights / counts_tok
    stats = jnp.sum(stats, axis=0)
    total, picked = stats.reshape(2, plane)
    lse = SOFTCAP + jnp.log(total)
    rows = jnp.stack([lse, coef, labels] + [jnp.zeros_like(lse)] * 5)

    split = half
    to_x = gradient_part(n, where_xy, rows, own_c, sib_c, unembed, unembed_sib, 0, split)
    to_y = gradient_part(n, where_yx, rows, own_c, sib_c, unembed, unembed_sib, split, width - split)
    to_y, lse, picked = lax.optimization_barrier((to_y, lse, picked))
    got_x = [to_x[0]] + [shifted(to_x[e], "x", -e) for e in range(1, n)]
    got_y = [to_y[0]] + [shifted(to_y[d], "y", -d) for d in range(1, n)]

    sums = by_x(weights * (lse - picked))
    sums = jnp.where(core == 0, sums, jnp.roll(sums, 1))
    losses = (sums + lax.ppermute(sums, "core", [(0, 1), (1, 0)])) / counts

    part_x, part_y = summed(got_x), summed(got_y)
    cut = lambda v, i: v[i * nz * own_rows : (i + 1) * nz * own_rows]
    got_y = [cut(part_x, 0)] + [shifted(cut(part_x, d), "y", -d) for d in range(1, n)]
    got_x = [cut(part_y, 0)] + [shifted(cut(part_y, e), "x", -e) for e in range(1, n)]
    part = jnp.concatenate([summed(got_y), summed(got_x)], axis=1).reshape(nz, own_rows, width)
    got = lax.all_to_all(part, "z", 0, 0, tiled=True)
    return jnp.sum(got.astype(f32), axis=0), losses


def solution(mesh):
    sections, groups = mesh.devices.shape
    chips = Mesh(mesh.devices.reshape(sections // 2, 2, 4, groups // 4), ALL)
    return jax.shard_map(
        body,
        mesh=chips,
        in_specs=(P(ALL, None), P(ALL, None), P(ALL), P(ALL), P()),
        out_specs=(P(ALL, None), P()),
        check_vma=False,
    )
```

```python
import functools

import jax
import jax.numpy as jnp
from jax import lax
from jax.experimental import pallas as pl
from jax.experimental.pallas import tpu as pltpu
from jax.sharding import Mesh, PartitionSpec as P

SOFTCAP = 30.0
TAIL = 128
ALL = ("x", "core", "y", "z")
VMEM_BYTES = 52 * 1024 * 1024


def shifted(v, axis, by):
    n = lax.axis_size(axis)
    return lax.ppermute(v, axis, [(i, (i + by) % n) for i in range(n)])


def column_chunks(width, most):
    chunk = next(c for c in (most, 128) if width % c == 0)
    return [(at, chunk) for at in range(0, width, chunk)]


def fetches(sources, buffers, sems, chunks, offset=0):
    return [
        [
            pltpu.make_async_copy(src.at[:, pl.ds(offset + at, size)], dst.at[:, pl.ds(at, size)], sems.at[j, k])
            for k, (at, size) in enumerate(chunks)
        ]
        for j, (src, dst) in enumerate(zip(sources, buffers))
    ]


def logits_kernel(n, where_ref, *refs):
    late = refs[:n]
    early = refs[n : 2 * n]
    own_ref, sib_ref, sums_ref, own_out, sib_out, own_u, sib_u, tok, acc, sems = refs[2 * n :]
    half = early[0].shape[1]
    rows = late[0].shape[0] // n
    chunks = column_chunks(2 * half, 1536)
    copies = fetches((own_ref, sib_ref), (own_u, sib_u), sems, chunks)
    for part in copies:
        for copy in part:
            copy.start()

    for e in range(n):
        for d in range(n):
            at = pl.multiple_of(where_ref[e * n + d] * rows, rows)
            tok[pl.ds(at, rows), half:] = late[e][d * rows : (d + 1) * rows, :half]
            tok[pl.ds(at, rows), :half] = early[d][e * rows : (e + 1) * rows, :]

    sums = 0.0
    for j, (u, out) in enumerate(((own_u, own_out), (sib_u, sib_out))):
        for k, (at, size) in enumerate(chunks):
            copies[j][k].wait()
            part = lax.dot_general(
                tok[:, at : at + size],
                u[:, at : at + size],
                (((1,), (1,)), ((), ())),
                preferred_element_type=jnp.float32,
            )
            if k:
                part = acc[...] + part
            acc[...] = part
        capped = SOFTCAP * jnp.tanh(acc[...] / SOFTCAP)
        out[...] = capped
        sums = sums + jnp.sum(jnp.exp(capped - SOFTCAP), axis=1, keepdims=True)
    sums_ref[...] = jnp.broadcast_to(sums, sums_ref.shape)


def capped_logits(where, late, early, own, sib):
    n = len(late)
    vocab, width = own.shape
    plane = n * late[0].shape[0]
    vmem, hbm = pl.BlockSpec(memory_space=pltpu.VMEM), pl.BlockSpec(memory_space=pltpu.HBM)
    capped = jax.ShapeDtypeStruct((plane, vocab), jnp.float32)
    sums = jax.ShapeDtypeStruct((plane, TAIL), jnp.float32)
    return pl.pallas_call(
        functools.partial(logits_kernel, n),
        out_shape=(sums, capped, capped),
        in_specs=[pl.BlockSpec(memory_space=pltpu.SMEM)] + [vmem] * (2 * n) + [hbm] * 2,
        out_specs=(vmem,) * 3,
        scratch_shapes=[
            pltpu.VMEM((vocab, width), jnp.bfloat16),
            pltpu.VMEM((vocab, width), jnp.bfloat16),
            pltpu.VMEM((plane, width), jnp.bfloat16),
            pltpu.VMEM((plane, vocab), jnp.float32),
            pltpu.SemaphoreType.DMA((2, len(column_chunks(width, 1536)))),
        ],
        compiler_params=pltpu.CompilerParams(vmem_limit_bytes=VMEM_BYTES),
        cost_estimate=pl.CostEstimate(
            flops=4 * plane * vocab * width, bytes_accessed=4 * vocab * width + 4 * plane * width, transcendentals=0
        ),
    )(where, *late, *early, own, sib)


def labels_kernel(n, where_ref, own_ref, sib_ref, sums_ref, own_c, sib_c, rows_ref, send_ref, own_tail, sib_tail):
    plane, vocab = own_c.shape
    rows = plane // (n * n)
    for i in range(n * n):
        here = slice(i * rows, (i + 1) * rows)
        own_tail[pl.ds(pl.multiple_of(where_ref[i] * rows, rows), rows), :] = own_ref[here, :].astype(jnp.float32)
        at = pl.ds(pl.multiple_of(where_ref[n * n + 2 + i] * rows, rows), rows)
        sib_tail[at, :] = sib_ref[here, :].astype(jnp.float32)
    labels = sib_tail[:, 0:1] + 256.0 * sib_tail[:, 1:2] + 65536.0 * sib_tail[:, 2:3]
    picked = 0.0
    for j, capped in enumerate((own_c, sib_c)):
        ids = where_ref[n * n + j] + lax.broadcasted_iota(jnp.int32, (plane, vocab), 1)
        hits = ids == labels.astype(jnp.int32)
        picked = picked + jnp.sum(jnp.where(hits, capped[...], 0.0), axis=1, keepdims=True)
    lane = lax.broadcasted_iota(jnp.int32, (plane, 8), 1)
    columns = jnp.zeros((plane, 8), jnp.float32)
    for i, column in enumerate((sums_ref[:, 0:1], picked, labels, sib_tail[:, 3:4], own_tail[:, 3:4])):
        columns = jnp.where(lane == i, column, columns)
    known = columns.T
    rows_ref[...] = known
    lanes = send_ref.shape[1]
    one = [known[i : i + 1, at : at + lanes] for i in range(2) for at in range(0, plane, lanes)]
    block = jnp.concatenate(one * (8 // len(one)), axis=0)
    for i in range(send_ref.shape[0] // 8):
        send_ref[i * 8 : (i + 1) * 8, :] = block


def labels_and_sums(n, peers, where, own_tail, sib_tail, sums, own_c, sib_c):
    plane = own_c.shape[0]
    vmem = pl.BlockSpec(memory_space=pltpu.VMEM)
    return pl.pallas_call(
        functools.partial(labels_kernel, n),
        out_shape=(
            jax.ShapeDtypeStruct((8, plane), jnp.float32),
            jax.ShapeDtypeStruct((peers * 2 * plane // 128, 128), jnp.float32),
        ),
        in_specs=[pl.BlockSpec(memory_space=pltpu.SMEM)] + [vmem] * 5,
        out_specs=(vmem, vmem),
        scratch_shapes=[pltpu.VMEM((plane, TAIL), jnp.float32)] * 2,
        compiler_params=pltpu.CompilerParams(vmem_limit_bytes=8 * 1024 * 1024),
    )(where, own_tail, sib_tail, sums, own_c, sib_c)


def gradient_kernel(n, where_ref, rows_ref, own_c, sib_c, own_ref, sib_ref, *refs):
    outs = refs[:n]
    own_p, sib_p, columns = refs[n:]
    plane, vocab = own_c.shape
    rows = plane // (n * n)

    @pl.when(pl.program_id(0) == 0)
    def _():
        columns[...] = rows_ref[...].T
        for i in range(n * n):
            at = pl.ds(pl.multiple_of(where_ref[i] * rows, rows), rows)
            to = slice(i * rows, (i + 1) * rows)
            known = columns[at, :]
            lse, coef, labels = known[:, 0:1], known[:, 1:2], known[:, 2:3].astype(jnp.int32)
            for c_ref, out, base in ((own_c, own_p, where_ref[n * n]), (sib_c, sib_p, where_ref[n * n + 1])):
                capped = c_ref[at, :]
                ids = base + lax.broadcasted_iota(jnp.int32, (rows, vocab), 1)
                grad = jnp.exp(capped - lse) - jnp.where(ids == labels, 1.0, 0.0)
                out[to, :] = (coef * grad * (1.0 - (capped / SOFTCAP) ** 2)).astype(jnp.bfloat16)

    part = jnp.dot(own_p[...], own_ref[...], preferred_element_type=jnp.float32)
    part = part + jnp.dot(sib_p[...], sib_ref[...], preferred_element_type=jnp.float32)
    part = part.astype(jnp.bfloat16)
    for i in range(n):
        outs[i][...] = part[i * n * rows : (i + 1) * n * rows, :]


def gradient_part(n, where, rows, own_c, sib_c, own, sib, start, size):
    plane, vocab = own_c.shape
    chunk = next(c for c in range(1152, 0, -128) if size % c == 0 and start % c == 0)
    steps, skip = size // chunk, start // chunk
    whole = lambda a: pl.BlockSpec(a.shape, lambda i: (0, 0))
    block = pl.BlockSpec((vocab, chunk), lambda i: (0, i + skip))
    piece = jax.ShapeDtypeStruct((plane // n, size), jnp.bfloat16)
    return pl.pallas_call(
        functools.partial(gradient_kernel, n),
        grid=(steps,),
        out_shape=(piece,) * n,
        in_specs=[pl.BlockSpec(memory_space=pltpu.SMEM), whole(rows), whole(own_c), whole(sib_c), block, block],
        out_specs=(pl.BlockSpec((plane // n, chunk), lambda i: (0, i)),) * n,
        scratch_shapes=[
            pltpu.VMEM((plane, vocab), jnp.bfloat16),
            pltpu.VMEM((plane, vocab), jnp.bfloat16),
            pltpu.VMEM((plane, 8), jnp.float32),
        ],
        compiler_params=pltpu.CompilerParams(vmem_limit_bytes=VMEM_BYTES),
        cost_estimate=pl.CostEstimate(
            flops=4 * plane * vocab * size, bytes_accessed=4 * vocab * size + 2 * plane * size, transcendentals=0
        ),
    )(where, rows, own_c, sib_c, own, sib)


def summed(pieces):
    return sum(p.astype(jnp.float32) for p in pieces).astype(jnp.bfloat16)


def body(hidden, unembed, targets, valid_mask, loss_scale):
    own_rows, width = hidden.shape
    vocab = unembed.shape[0]
    nx, _, ny, nz = (lax.axis_size(a) for a in ALL)
    n = nx
    ix, core, iy, iz = (lax.axis_index(a) for a in ALL)
    plane = nx * ny * nz * own_rows
    per_x = plane // nx
    half = width // 2
    f32, i32 = jnp.float32, jnp.int32

    unembed_sib = lax.ppermute(unembed, "core", [(0, 1), (1, 0)])

    digits = jnp.stack([targets % 256, (targets // 256) % 256, targets // 65536, valid_mask], axis=1)
    tail = jnp.pad(digits, ((0, 0), (0, TAIL - digits.shape[1]))).astype(jnp.bfloat16)
    for_all = lambda v: jnp.broadcast_to(v[None], (nz, *v.shape))
    mine = jnp.concatenate([for_all(hidden), for_all(tail)], axis=2)
    by_z = lax.all_to_all(mine, "z", 0, 0, tiled=True).reshape(nz * own_rows, width + TAIL)
    by_z, unembed_sib = lax.optimization_barrier((by_z, unembed_sib))

    first, second = by_z[:, :half], by_z[:, half:]
    along_x = jnp.concatenate([first] + [shifted(first, "x", e) for e in range(1, n)])
    along_y = jnp.concatenate([second] + [shifted(second, "y", d) for d in range(1, n)])
    late = [along_y] + [shifted(along_y, "x", e) for e in range(1, n)]
    early = [along_x] + [shifted(along_x, "y", d) for d in range(1, n)]
    tail_own = jnp.concatenate([v[:, half:] for v in late])
    tail_sib = lax.ppermute(tail_own, "core", [(0, 1), (1, 0)])

    device = lax.axis_index(ALL)
    bases = vocab * jnp.stack([device, device + (1 - 2 * core) * ny * nz])
    near_x, near_y = (ix - jnp.arange(nx)) % nx, (iy - jnp.arange(ny)) % ny
    places = near_x[:, None] * ny + near_y[None, :]
    label_places = ((near_x - core) % nx)[:, None] * ny + near_y[None, :]
    where_xy = jnp.concatenate([places.ravel(), bases, label_places.ravel()]).astype(i32)
    where_yx = jnp.concatenate([places.T.ravel(), bases]).astype(i32)

    sums, own_c, sib_c = capped_logits(where_xy, late, early, unembed, unembed_sib)
    peers, lines = nx * ny * nz, 2 * plane // 128
    known, send = labels_and_sums(n, peers, where_xy, tail_own, tail_sib, sums, own_c, sib_c)
    stats = lax.all_to_all(send.reshape(peers, lines, 128), ("x", "y", "z"), 0, 0, tiled=True)
    labels, weights = known[2], known[3]
    by_x = lambda v: jnp.sum(v.reshape(nx, per_x), axis=1)
    of_tokens = by_x(weights)
    counts = by_x(known[4]) + jnp.where(core == 0, of_tokens, jnp.roll(of_tokens, 1))
    counts_tok = jnp.repeat(jnp.where(core == 0, counts, jnp.roll(counts, -1)), per_x)
    coef = loss_scale * weights / counts_tok
    stats = jnp.sum(stats, axis=0)
    total, picked = stats.reshape(2, plane)
    lse = SOFTCAP + jnp.log(total)
    rows = jnp.stack([lse, coef, labels] + [jnp.zeros_like(lse)] * 5)

    split = half
    to_x = gradient_part(n, where_xy, rows, own_c, sib_c, unembed, unembed_sib, 0, split)
    to_y = gradient_part(n, where_yx, rows, own_c, sib_c, unembed, unembed_sib, split, width - split)
    to_y, lse, picked = lax.optimization_barrier((to_y, lse, picked))
    got_x = [to_x[0]] + [shifted(to_x[e], "x", -e) for e in range(1, n)]
    got_y = [to_y[0]] + [shifted(to_y[d], "y", -d) for d in range(1, n)]

    sums = by_x(weights * (lse - picked))
    sums = jnp.where(core == 0, sums, jnp.roll(sums, 1))
    losses = (sums + lax.ppermute(sums, "core", [(0, 1), (1, 0)])) / counts

    part_x, part_y = summed(got_x), summed(got_y)
    cut = lambda v, i: v[i * nz * own_rows : (i + 1) * nz * own_rows]
    got_y = [cut(part_x, 0)] + [shifted(cut(part_x, d), "y", -d) for d in range(1, n)]
    got_x = [cut(part_y, 0)] + [shifted(cut(part_y, e), "x", -e) for e in range(1, n)]
    part = jnp.concatenate([summed(got_y), summed(got_x)], axis=1).reshape(nz, own_rows, width)
    got = lax.all_to_all(part, "z", 0, 0, tiled=True)
    return jnp.sum(got.astype(f32), axis=0), losses


def solution(mesh):
    sections, groups = mesh.devices.shape
    chips = Mesh(mesh.devices.reshape(sections // 2, 2, 4, groups // 4), ALL)
    return jax.shard_map(
        body,
        mesh=chips,
        in_specs=(P(ALL, None), P(ALL, None), P(ALL), P(ALL), P()),
        out_specs=(P(ALL, None), P()),
        check_vma=False,
    )
```

```python
import functools

import jax
import jax.numpy as jnp
from jax import lax
from jax.experimental import pallas as pl
from jax.experimental.pallas import tpu as pltpu
from jax.sharding import Mesh, PartitionSpec as P

SOFTCAP = 30.0
TAIL = 128
ALL = ("x", "core", "y", "z")
VMEM_BYTES = 52 * 1024 * 1024


def shifted(v, axis, by):
    n = lax.axis_size(axis)
    return lax.ppermute(v, axis, [(i, (i + by) % n) for i in range(n)])


def column_chunks(width, most):
    chunk = next(c for c in (most, 128) if width % c == 0)
    return [(at, chunk) for at in range(0, width, chunk)]


def fetches(sources, buffers, sems, chunks, offset=0):
    return [
        [
            pltpu.make_async_copy(src.at[:, pl.ds(offset + at, size)], dst.at[:, pl.ds(at, size)], sems.at[j, k])
            for k, (at, size) in enumerate(chunks)
        ]
        for j, (src, dst) in enumerate(zip(sources, buffers))
    ]


def logits_kernel(n, where_ref, *refs):
    late = refs[:n]
    early = refs[n : 2 * n]
    own_ref, sib_ref, sums_ref, own_out, sib_out, own_u, sib_u, tok, acc, sems = refs[2 * n :]
    half = early[0].shape[1]
    rows = late[0].shape[0] // n
    chunks = column_chunks(2 * half, 1536)
    copies = fetches((own_ref, sib_ref), (own_u, sib_u), sems, chunks)
    for part in copies:
        for copy in part:
            copy.start()

    for e in range(n):
        for d in range(n):
            at = pl.multiple_of(where_ref[e * n + d] * rows, rows)
            tok[pl.ds(at, rows), half:] = late[e][d * rows : (d + 1) * rows, :half]
            tok[pl.ds(at, rows), :half] = early[d][e * rows : (e + 1) * rows, :]

    sums = 0.0
    for j, (u, out) in enumerate(((own_u, own_out), (sib_u, sib_out))):
        for k, (at, size) in enumerate(chunks):
            copies[j][k].wait()
            part = lax.dot_general(
                tok[:, at : at + size],
                u[:, at : at + size],
                (((1,), (1,)), ((), ())),
                preferred_element_type=jnp.float32,
            )
            if k:
                part = acc[...] + part
            acc[...] = part
        capped = SOFTCAP * jnp.tanh(acc[...] / SOFTCAP)
        out[...] = capped
        sums = sums + jnp.sum(jnp.exp(capped - SOFTCAP), axis=1, keepdims=True)
    sums_ref[...] = jnp.broadcast_to(sums, sums_ref.shape)


def capped_logits(where, late, early, own, sib):
    n = len(late)
    vocab, width = own.shape
    plane = n * late[0].shape[0]
    vmem, hbm = pl.BlockSpec(memory_space=pltpu.VMEM), pl.BlockSpec(memory_space=pltpu.HBM)
    capped = jax.ShapeDtypeStruct((plane, vocab), jnp.float32)
    sums = jax.ShapeDtypeStruct((plane, TAIL), jnp.float32)
    return pl.pallas_call(
        functools.partial(logits_kernel, n),
        out_shape=(sums, capped, capped),
        in_specs=[pl.BlockSpec(memory_space=pltpu.SMEM)] + [vmem] * (2 * n) + [hbm] * 2,
        out_specs=(vmem,) * 3,
        scratch_shapes=[
            pltpu.VMEM((vocab, width), jnp.bfloat16),
            pltpu.VMEM((vocab, width), jnp.bfloat16),
            pltpu.VMEM((plane, width), jnp.bfloat16),
            pltpu.VMEM((plane, vocab), jnp.float32),
            pltpu.SemaphoreType.DMA((2, len(column_chunks(width, 1536)))),
        ],
        compiler_params=pltpu.CompilerParams(vmem_limit_bytes=VMEM_BYTES),
        cost_estimate=pl.CostEstimate(
            flops=4 * plane * vocab * width, bytes_accessed=4 * vocab * width + 4 * plane * width, transcendentals=0
        ),
    )(where, *late, *early, own, sib)


def labels_kernel(n, where_ref, own_ref, sib_ref, sums_ref, own_c, sib_c, rows_ref, send_ref, own_tail, sib_tail):
    plane, vocab = own_c.shape
    rows = plane // (n * n)
    for i in range(n * n):
        here = slice(i * rows, (i + 1) * rows)
        own_tail[pl.ds(pl.multiple_of(where_ref[i] * rows, rows), rows), :] = own_ref[here, :].astype(jnp.float32)
        at = pl.ds(pl.multiple_of(where_ref[n * n + 2 + i] * rows, rows), rows)
        sib_tail[at, :] = sib_ref[here, :].astype(jnp.float32)
    labels = sib_tail[:, 0:1] + 256.0 * sib_tail[:, 1:2] + 65536.0 * sib_tail[:, 2:3]
    picked = 0.0
    for j, capped in enumerate((own_c, sib_c)):
        ids = where_ref[n * n + j] + lax.broadcasted_iota(jnp.int32, (plane, vocab), 1)
        hits = ids == labels.astype(jnp.int32)
        picked = picked + jnp.sum(jnp.where(hits, capped[...], 0.0), axis=1, keepdims=True)
    lane = lax.broadcasted_iota(jnp.int32, (plane, 8), 1)
    columns = jnp.zeros((plane, 8), jnp.float32)
    for i, column in enumerate((sums_ref[:, 0:1], picked, labels, sib_tail[:, 3:4], own_tail[:, 3:4])):
        columns = jnp.where(lane == i, column, columns)
    known = columns.T
    rows_ref[...] = known
    lanes = send_ref.shape[1]
    one = [known[i : i + 1, at : at + lanes] for i in range(2) for at in range(0, plane, lanes)]
    block = jnp.concatenate(one * (8 // len(one)), axis=0)
    for i in range(send_ref.shape[0] // 8):
        send_ref[i * 8 : (i + 1) * 8, :] = block


def labels_and_sums(n, peers, where, own_tail, sib_tail, sums, own_c, sib_c):
    plane = own_c.shape[0]
    vmem = pl.BlockSpec(memory_space=pltpu.VMEM)
    return pl.pallas_call(
        functools.partial(labels_kernel, n),
        out_shape=(
            jax.ShapeDtypeStruct((8, plane), jnp.float32),
            jax.ShapeDtypeStruct((peers * 2 * plane // 128, 128), jnp.float32),
        ),
        in_specs=[pl.BlockSpec(memory_space=pltpu.SMEM)] + [vmem] * 5,
        out_specs=(vmem, vmem),
        scratch_shapes=[pltpu.VMEM((plane, TAIL), jnp.float32)] * 2,
        compiler_params=pltpu.CompilerParams(vmem_limit_bytes=60 * 1024 * 1024),
    )(where, own_tail, sib_tail, sums, own_c, sib_c)


def gradient_kernel(n, where_ref, rows_ref, own_c, sib_c, own_ref, sib_ref, *refs):
    outs = refs[:n]
    own_p, sib_p, columns = refs[n:]
    plane, vocab = own_c.shape
    rows = plane // (n * n)

    @pl.when(pl.program_id(0) == 0)
    def _():
        columns[...] = rows_ref[...].T
        for i in range(n * n):
            at = pl.ds(pl.multiple_of(where_ref[i] * rows, rows), rows)
            to = slice(i * rows, (i + 1) * rows)
            known = columns[at, :]
            lse, coef, labels = known[:, 0:1], known[:, 1:2], known[:, 2:3].astype(jnp.int32)
            for c_ref, out, base in ((own_c, own_p, where_ref[n * n]), (sib_c, sib_p, where_ref[n * n + 1])):
                capped = c_ref[at, :]
                ids = base + lax.broadcasted_iota(jnp.int32, (rows, vocab), 1)
                grad = jnp.exp(capped - lse) - jnp.where(ids == labels, 1.0, 0.0)
                out[to, :] = (coef * grad * (1.0 - (capped / SOFTCAP) ** 2)).astype(jnp.bfloat16)

    part = jnp.dot(own_p[...], own_ref[...], preferred_element_type=jnp.float32)
    part = part + jnp.dot(sib_p[...], sib_ref[...], preferred_element_type=jnp.float32)
    part = part.astype(jnp.bfloat16)
    for i in range(n):
        outs[i][...] = part[i * n * rows : (i + 1) * n * rows, :]


def gradient_part(n, where, rows, own_c, sib_c, own, sib, start, size):
    plane, vocab = own_c.shape
    chunk = next(c for c in range(1152, 0, -128) if size % c == 0 and start % c == 0)
    steps, skip = size // chunk, start // chunk
    whole = lambda a: pl.BlockSpec(a.shape, lambda i: (0, 0))
    block = pl.BlockSpec((vocab, chunk), lambda i: (0, i + skip))
    piece = jax.ShapeDtypeStruct((plane // n, size), jnp.bfloat16)
    return pl.pallas_call(
        functools.partial(gradient_kernel, n),
        grid=(steps,),
        out_shape=(piece,) * n,
        in_specs=[pl.BlockSpec(memory_space=pltpu.SMEM), whole(rows), whole(own_c), whole(sib_c), block, block],
        out_specs=(pl.BlockSpec((plane // n, chunk), lambda i: (0, i)),) * n,
        scratch_shapes=[
            pltpu.VMEM((plane, vocab), jnp.bfloat16),
            pltpu.VMEM((plane, vocab), jnp.bfloat16),
            pltpu.VMEM((plane, 8), jnp.float32),
        ],
        compiler_params=pltpu.CompilerParams(vmem_limit_bytes=VMEM_BYTES),
        cost_estimate=pl.CostEstimate(
            flops=4 * plane * vocab * size, bytes_accessed=4 * vocab * size + 2 * plane * size, transcendentals=0
        ),
    )(where, rows, own_c, sib_c, own, sib)


def summed(pieces):
    return sum(p.astype(jnp.float32) for p in pieces).astype(jnp.bfloat16)


def body(hidden, unembed, targets, valid_mask, loss_scale):
    own_rows, width = hidden.shape
    vocab = unembed.shape[0]
    nx, _, ny, nz = (lax.axis_size(a) for a in ALL)
    n = nx
    ix, core, iy, iz = (lax.axis_index(a) for a in ALL)
    plane = nx * ny * nz * own_rows
    per_x = plane // nx
    half = width // 2
    f32, i32 = jnp.float32, jnp.int32

    unembed_sib = lax.ppermute(unembed, "core", [(0, 1), (1, 0)])

    digits = jnp.stack([targets % 256, (targets // 256) % 256, targets // 65536, valid_mask], axis=1)
    tail = jnp.pad(digits, ((0, 0), (0, TAIL - digits.shape[1]))).astype(jnp.bfloat16)
    for_all = lambda v: jnp.broadcast_to(v[None], (nz, *v.shape))
    mine = jnp.concatenate([for_all(hidden), for_all(tail)], axis=2)
    by_z = lax.all_to_all(mine, "z", 0, 0, tiled=True).reshape(nz * own_rows, width + TAIL)
    by_z, unembed_sib = lax.optimization_barrier((by_z, unembed_sib))

    first, second = by_z[:, :half], by_z[:, half:]
    along_x = jnp.concatenate([first] + [shifted(first, "x", e) for e in range(1, n)])
    along_y = jnp.concatenate([second] + [shifted(second, "y", d) for d in range(1, n)])
    late = [along_y] + [shifted(along_y, "x", e) for e in range(1, n)]
    early = [along_x] + [shifted(along_x, "y", d) for d in range(1, n)]
    tail_own = jnp.concatenate([v[:, half:] for v in late])
    tail_sib = lax.ppermute(tail_own, "core", [(0, 1), (1, 0)])

    device = lax.axis_index(ALL)
    bases = vocab * jnp.stack([device, device + (1 - 2 * core) * ny * nz])
    near_x, near_y = (ix - jnp.arange(nx)) % nx, (iy - jnp.arange(ny)) % ny
    places = near_x[:, None] * ny + near_y[None, :]
    label_places = ((near_x - core) % nx)[:, None] * ny + near_y[None, :]
    where_xy = jnp.concatenate([places.ravel(), bases, label_places.ravel()]).astype(i32)
    where_yx = jnp.concatenate([places.T.ravel(), bases]).astype(i32)

    sums, own_c, sib_c = capped_logits(where_xy, late, early, unembed, unembed_sib)
    peers, lines = nx * ny * nz, 2 * plane // 128
    known, send = labels_and_sums(n, peers, where_xy, tail_own, tail_sib, sums, own_c, sib_c)
    stats = lax.all_to_all(send.reshape(peers, lines, 128), ("x", "y", "z"), 0, 0, tiled=True)
    labels, weights = known[2], known[3]
    by_x = lambda v: jnp.sum(v.reshape(nx, per_x), axis=1)
    of_tokens = by_x(weights)
    counts = by_x(known[4]) + jnp.where(core == 0, of_tokens, jnp.roll(of_tokens, 1))
    counts_tok = jnp.repeat(jnp.where(core == 0, counts, jnp.roll(counts, -1)), per_x)
    coef = loss_scale * weights / counts_tok
    stats = jnp.sum(stats, axis=0)
    total, picked = stats.reshape(2, plane)
    lse = SOFTCAP + jnp.log(total)
    rows = jnp.stack([lse, coef, labels] + [jnp.zeros_like(lse)] * 5)

    split = half
    to_x = gradient_part(n, where_xy, rows, own_c, sib_c, unembed, unembed_sib, 0, split)
    to_y = gradient_part(n, where_yx, rows, own_c, sib_c, unembed, unembed_sib, split, width - split)
    to_y, lse, picked = lax.optimization_barrier((to_y, lse, picked))
    got_x = [to_x[0]] + [shifted(to_x[e], "x", -e) for e in range(1, n)]
    got_y = [to_y[0]] + [shifted(to_y[d], "y", -d) for d in range(1, n)]

    sums = by_x(weights * (lse - picked))
    sums = jnp.where(core == 0, sums, jnp.roll(sums, 1))
    losses = (sums + lax.ppermute(sums, "core", [(0, 1), (1, 0)])) / counts

    part_x, part_y = summed(got_x), summed(got_y)
    cut = lambda v, i: v[i * nz * own_rows : (i + 1) * nz * own_rows]
    got_y = [cut(part_x, 0)] + [shifted(cut(part_x, d), "y", -d) for d in range(1, n)]
    got_x = [cut(part_y, 0)] + [shifted(cut(part_y, e), "x", -e) for e in range(1, n)]
    part = jnp.concatenate([summed(got_y), summed(got_x)], axis=1).reshape(nz, own_rows, width)
    got = lax.all_to_all(part, "z", 0, 0, tiled=True)
    return jnp.sum(got.astype(f32), axis=0), losses


def solution(mesh):
    sections, groups = mesh.devices.shape
    chips = Mesh(mesh.devices.reshape(sections // 2, 2, 4, groups // 4), ALL)
    return jax.shard_map(
        body,
        mesh=chips,
        in_specs=(P(ALL, None), P(ALL, None), P(ALL), P(ALL), P()),
        out_specs=(P(ALL, None), P()),
        check_vma=False,
    )
```
